768 devices in a mesh: rep: 16 (over y, core), grp: 48 (over z, x).
Axes of the slice: x: 4, y: 8, z: 12, core: 2. Of those that a mesh axis runs over, the one named last changes fastest.
Arguments:
- grad_terms: bfloat16 [16, 48, 384, 4096], P('rep', 'grp'), may hold values from -5 to 5
- error_buffer: float32 [16, 384, 4096], P('rep', 'grp'), may hold values from -6 to 6
- weight: float32 [384, 4096], P('grp'), may hold values from -6 to 6
- q_prev: float32 [4096, 64], replicated, may hold values from -0.09375 to 0.09375
Outputs:
- q_next: float32 [4096, 64], replicated
- error_next: float32 [16, 384, 4096], P('rep', 'grp')
- weight_next: float32 [384, 4096], P('grp')
The draws below stay inside these ranges and needn't reach their ends.
All inputs are finite; a program needn't handle non-finite values.
Results may differ from the reference program's by a relative error of at most 0.0003.
Values sent between devices are 32-bit elements; how exact they have to be, the bound alone decides.
No kernel may reach another device: no remote copies, remote signals or barrier semaphores. Data moves between devices by JAX's collectives and lax.ppermute only.
A program may use at most 32 MiB of HBM per device.

```python
import jax
import jax.numpy as jnp
from jax import lax

D = 4096
RANK = 64
ROWS = 384
N_REP = 16
N_GRP = 48


def raised(entries, stream_key, source, target, shards_of, factor):
    def block_of(axis_at):
        return (jnp.arange(entries.shape[axis_at]) // (entries.shape[axis_at] // shards_of)).reshape((-1,) + (1,) * (entries.ndim - 1 - axis_at))

    near = jax.random.permutation(stream_key, shards_of)[block_of(target)]
    other_side = (block_of(target) + shards_of // 2) % shards_of
    return jnp.where((block_of(source) == near) | (block_of(source) == other_side), factor * entries, entries)


def steps_of(own_key, shape, pieces, low, high):
    def one(axis_at, blocks):
        steps = jax.random.uniform(jax.random.fold_in(jax.random.fold_in(own_key, 6), axis_at), (blocks,), jnp.float32, low / len(pieces), high / len(pieces))
        return jnp.repeat(jnp.exp(steps), shape[axis_at] // blocks).reshape((-1,) + (1,) * (len(shape) - axis_at - 1))

    loudness = one(*pieces[0])
    for cut in pieces[1:]:
        loudness = loudness * one(*cut)
    return loudness


def normal_values(own_key, shape, scale, most, cuts=(), kind=jnp.bfloat16):
    factor_of = steps_of(own_key, shape, cuts, -0.22, 0.18) if cuts else 1.0
    drawn = jax.random.normal(own_key, shape, jnp.float32) * scale * factor_of
    return jnp.minimum(jnp.maximum(drawn, -most), most).astype(kind)


def heavy_noise(rng, extent, scale, bound, shards, heavy, kind=jnp.bfloat16):
    drawn = scale * jax.random.normal(rng, extent, jnp.float32)
    if shards:
        drawn = drawn * steps_of(rng, extent, shards, -0.22, 0.18)
    return jnp.clip(raised(drawn, jax.random.fold_in(rng, 3), *heavy), -bound, bound).astype(kind)


def setup_inputs(seed: int = 0) -> dict:
    key_of = jax.random.split(jax.random.key(seed), 5)
    grad_terms = heavy_noise(key_of[0], (N_REP, N_GRP, ROWS, D), 0.15, 5.0, ((0, 16), (1, 48)), (1, 2, 48, 3.25))
    error_buffer = normal_values(key_of[1], (N_REP, ROWS, D), 0.5, 6.0, ((0, 16), (1, 48)), jnp.float32)
    weight = normal_values(key_of[2], (ROWS, D), 1.0, 6.0, ((0, 48),), jnp.float32)
    q_prev = normal_values(key_of[3], (D, RANK), D ** -0.5, 0.09375, (), jnp.float32)
    return {"grad_terms": grad_terms, "error_buffer": error_buffer, "weight": weight, "q_prev": q_prev}


def orthonormal(left):
    gram = jnp.dot(left.T, left, precision=lax.Precision.HIGHEST)
    shift = 0.01 * (jnp.trace(gram) / RANK + 1e-06)
    shifted = gram + shift * jnp.eye(RANK, dtype=gram.dtype)
    lower = jnp.linalg.cholesky(shifted)
    return lax.linalg.triangular_solve(lower, left, left_side=False, lower=True, transpose_a=True)

def reference(grad_terms, error_buffer, weight, q_prev):

    def group_total(terms):
        return jnp.sum(terms.astype(jnp.float32), axis=0)
    group_grad = lax.map(group_total, grad_terms)
    corrected = group_grad + error_buffer
    left = jnp.einsum('rij,jk->ik', corrected, q_prev, precision=lax.Precision.HIGHEST)
    left_hat = orthonormal(left)
    q_next = jnp.einsum('rij,ik->jk', corrected, left_hat, precision=lax.Precision.HIGHEST) / N_REP
    approx = jnp.dot(left_hat, q_next.T, precision=lax.Precision.HIGHEST)
    error_next = corrected - approx[None]
    weight_next = weight - 0.5 * approx
    return (q_next, error_next, weight_next)
```

```python
import jax
import jax.numpy as jnp
from jax import lax
from jax.sharding import Mesh, PartitionSpec as P

NY, NC, NZ, NX = 8, 2, 12, 4
REP, GRP = ("y", "core"), ("z", "x")
F32, BF16 = jnp.float32, jnp.bfloat16


def full_dot(left, right):
    return jnp.dot(left, right, precision=lax.Precision.HIGHEST)


def parts_of(value):
    high = lax.reduce_precision(value, 8, 7)
    rest = value - high
    middle = lax.reduce_precision(rest, 8, 7)
    return [p.astype(BF16) for p in (high, middle, rest - middle)]


def exchange(value, axes):
    return lax.all_to_all(value, axes, 0, 0, tiled=True)


def gathered(value, axes, n):
    return exchange(jnp.broadcast_to(value[None], (n,) + value.shape), axes)


def scatter(value, axis):
    return lax.psum_scatter(value, axis, scatter_dimension=0, tiled=True)


def on_device(grad_terms, error_buffer, weight, q_prev):
    term, error = grad_terms[0, 0], error_buffer[0]
    rows, width = term.shape
    rank = q_prev.shape[1]
    n_rep, n_grp = NY * NC, NZ * NX
    own = rows // n_grp
    at = (lax.axis_index("z") * NX + lax.axis_index("x")) * own

    half = width // 2
    first = term[:, :half].reshape(NZ, NX, own, half).transpose(1, 0, 2, 3)
    first = scatter(first.reshape(rows, half).astype(F32), "x")
    second = scatter(term[:, half:].astype(F32), "z")
    first = scatter(first, "z")
    second = scatter(second, "x")

    q_parts = jnp.concatenate(parts_of(q_prev.T), axis=0)
    left = lax.dot_general(term, q_parts, (((1,), (1,)), ((), ())), preferred_element_type=F32)
    left = left[:, :rank] + left[:, rank : 2 * rank] + left[:, 2 * rank :]
    mine = lax.dynamic_slice_in_dim(left, at, own, 0) + full_dot(error, q_prev)
    left = lax.dynamic_update_slice_in_dim(left, mine, at, 0)
    block = exchange(left.reshape(n_rep, rows // n_rep, rank), REP).sum(0)
    block = gathered(block, GRP, n_grp).sum(0)
    left = gathered(block, REP, n_rep).reshape(rows, rank)
    left_own = lax.dynamic_slice_in_dim(left, at, own, 0)

    turned = parts_of(left.T)
    right = sum(jnp.dot(p, term, preferred_element_type=F32) for p in turned)
    right = right + full_dot(left_own.T, error)
    cols = width // n_rep
    right = right.reshape(rank, n_rep, cols).transpose(1, 0, 2)
    right = exchange(right, REP).sum(0)
    lanes = 128
    flat = right.reshape(rank, cols // lanes, lanes).transpose(1, 0, 2)
    flat = flat.reshape(rank * cols // lanes, lanes)
    pieces = -(-flat.shape[0] // n_grp)
    flat = jnp.pad(flat, ((0, pieces * n_grp - flat.shape[0]), (0, 0)))
    piece = exchange(flat.reshape(n_grp, pieces, lanes), GRP).sum(0)
    flat = gathered(piece, GRP, n_grp).reshape(n_grp * pieces, lanes)
    flat = flat[: rank * cols // lanes].reshape(cols // lanes, rank, lanes)
    right = flat.transpose(1, 0, 2).reshape(rank, cols)

    gram = full_dot(left.T, left)
    shift = 0.01 * (jnp.trace(gram) / rank + 1e-06)
    eye = jnp.eye(rank, dtype=F32)
    lower = jnp.linalg.cholesky(gram + shift * eye)
    inverse = lax.linalg.triangular_solve(lower, eye, left_side=True, lower=True)

    right = full_dot(inverse, right) / n_rep
    q_turned = gathered(right, REP, n_rep).transpose(1, 0, 2).reshape(rank, width)
    left_hat = full_dot(left_own, inverse.T)
    approx = full_dot(left_hat, q_turned)
    corrected = jnp.concatenate([first, second], axis=1) + error
    return (q_turned.T, (corrected - approx)[None], weight - 0.5 * approx)


def solution(mesh):
    split = Mesh(mesh.devices.reshape(NY, NC, NZ, NX), REP + GRP)
    placed = (P(REP, GRP, None, None), P(REP, GRP, None), P(GRP, None), P())
    return jax.shard_map(
        on_device,
        mesh=split,
        in_specs=placed,
        out_specs=(P(), P(REP, GRP, None), P(GRP, None)),
        check_vma=False,
    )
```

```python
import functools

import jax
import jax.numpy as jnp
from jax import lax
from jax.experimental import pallas as pl
from jax.experimental.pallas import tpu as pltpu
from jax.sharding import Mesh, PartitionSpec as P

NY, NC, NZ, NX = 8, 2, 12, 4
REP, GRP = ("y", "core"), ("z", "x")
F32, BF16 = jnp.float32, jnp.bfloat16
RANK, OWN, LANES = 64, 8, 128
HIGHEST = lax.Precision.HIGHEST
MIB = 2**20


def full_dot(left, right):
    return jnp.dot(left, right, precision=HIGHEST)


def parts_of(value):
    high = value.astype(BF16).astype(F32)
    rest = value - high
    middle = rest.astype(BF16).astype(F32)
    return [high, middle, rest - middle]


def stacked(parts):
    return jnp.concatenate(parts, axis=0).astype(BF16)


def dot_nt(left, right):
    return lax.dot_general(left, right, (((1,), (1,)), ((), ())), preferred_element_type=F32)


def exchange(value, axes):
    return lax.all_to_all(value, axes, 0, 0, tiled=True)


def gathered(value, axes, n):
    return exchange(jnp.broadcast_to(value[None], (n,) + value.shape), axes)


def scatter(value, axis):
    return lax.psum_scatter(value, axis, scatter_dimension=0, tiled=True)


def swap(value):
    return lax.ppermute(value, "core", [(i, NC - 1 - i) for i in range(NC)])


def slot_of(tile):
    n_rep = NY * NC
    return tile % n_rep, tile // n_rep * OWN


def own_place(g, n_tiles):
    low = g < n_tiles
    return low, pl.multiple_of(jnp.where(low, g, g - n_tiles) * OWN, OWN)


def prepare(g_ref, term_ref, error_ref, q_ref, wide_ref, left_ref, parts, packed):
    step = pl.program_id(0)
    rows = term_ref.shape[0]

    @pl.when(step == 0)
    def _():
        for i, part in enumerate(parts_of(q_ref[...])):
            parts[i * RANK : (i + 1) * RANK] = part.astype(BF16)

    block = term_ref[...]
    for z in range(rows // (NX * OWN)):
        band = block[z * NX * OWN : (z + 1) * NX * OWN].astype(F32)
        for x in range(NX):
            wide_ref[x, z] = band[x * OWN : (x + 1) * OWN]
    product = dot_nt(block, parts[...])
    left = product[:, :RANK] + product[:, RANK : 2 * RANK] + product[:, 2 * RANK :]

    @pl.when(step == 0)
    def _():
        packed[:, :RANK] = left

    @pl.when(step == 1)
    def _():
        packed[:, RANK:] = left
        high, middle, low = parts_of(error_ref[...])
        errors = stacked([high, middle, low, jnp.zeros_like(low)])
        cross = dot_nt(errors, parts[...])
        own = cross[2 * OWN : 3 * OWN, :RANK] + cross[:OWN, 2 * RANK :]
        own = own + cross[OWN : 2 * OWN, RANK : 2 * RANK]
        own = own + cross[OWN : 2 * OWN, :RANK] + cross[:OWN, RANK : 2 * RANK]
        own = own + cross[:OWN, :RANK]
        n_tiles = rows // OWN
        first, at = own_place(g_ref[0], n_tiles)
        none = jnp.zeros_like(own)
        pair = jnp.concatenate([jnp.where(first, own, none), jnp.where(first, none, own)], axis=1)
        packed[pl.ds(at, OWN), :] += pair
        left_ref[...] = jnp.zeros_like(left_ref)
        for tile in range(n_tiles):
            device, slot = slot_of(tile)
            left_ref[device, slot : slot + OWN] = packed[tile * OWN : (tile + 1) * OWN]


def right_terms(s_ref, left_ref, term_ref, error_ref, send_ref, keep_ref, own_ref, packed, parts):
    step = pl.program_id(0)
    half = term_ref.shape[0] // 2
    n_tiles = half // OWN
    first, at = own_place(s_ref[0], n_tiles)

    @pl.when(step == 0)
    def _():
        for tile in range(n_tiles):
            device, slot = slot_of(tile)
            packed[tile * OWN : (tile + 1) * OWN] = left_ref[device, slot : slot + OWN]
        turned = packed[...].T
        for i in range(2):
            for j, part in enumerate(parts_of(turned[i * RANK : (i + 1) * RANK])):
                parts[i, j * RANK : (j + 1) * RANK] = part.astype(BF16)
        pair = packed[pl.ds(at, OWN), :]
        own_ref[...] = jnp.where(first, pair[:, :RANK], pair[:, RANK:])

    total = jnp.dot(parts[0], term_ref[:half], preferred_element_type=F32)
    total = total + jnp.dot(parts[1], term_ref[half:], preferred_element_type=F32)
    total = total[:RANK] + total[RANK : 2 * RANK] + total[2 * RANK :]
    total = total + lax.dot_general(
        own_ref[...], error_ref[...], (((0,), (0,)), ((), ())), precision=HIGHEST, preferred_element_type=F32
    )
    count, cols = send_ref.shape[0], send_ref.shape[2]

    @pl.when(step < 2)
    def _():
        for k in range(count):
            send_ref[k] = total[:, k * cols : (k + 1) * cols]

    @pl.when(step >= 2)
    def _():
        for k in range(count):
            keep_ref[k] = total[:, k * cols : (k + 1) * cols]


def fold(blocks_ref, _, flat_ref):
    total = blocks_ref[0]
    for i in range(1, blocks_ref.shape[0]):
        total = total + blocks_ref[i]
    flat_ref[...] = jnp.zeros_like(flat_ref)
    for i in range(total.shape[1] // LANES):
        flat_ref[i * RANK : (i + 1) * RANK] = total[:, i * LANES : (i + 1) * LANES]


def finish(s_ref, mine_ref, other_ref, left_ref, summed_ref, error_ref, weight_ref, q_ref, error_out, weight_out):
    step = pl.program_id(0)
    cols = mine_ref.shape[2]

    def run(blocks_ref):
        for k in range(blocks_ref.shape[0]):
            at = slice(k * cols, (k + 1) * cols)
            block = blocks_ref[k]
            q_ref[:, at] = block
            approx = jnp.dot(left_ref[...], block, precision=HIGHEST, preferred_element_type=F32)
            error_out[:, at] = summed_ref[:, at] + error_ref[:, at] - approx
            weight_out[:, at] = weight_ref[:, at] - 0.5 * approx

    pl.when(step == s_ref[1])(functools.partial(run, mine_ref))
    pl.when(step != s_ref[1])(functools.partial(run, other_ref))


def call(kernel, room, grid, in_specs, out_specs, out_shape, scratch=()):
    return pl.pallas_call(
        kernel,
        out_shape=out_shape,
        grid_spec=pltpu.PrefetchScalarGridSpec(
            num_scalar_prefetch=1, grid=grid, in_specs=in_specs, out_specs=out_specs, scratch_shapes=list(scratch)
        ),
        compiler_params=pltpu.CompilerParams(vmem_limit_bytes=room * MIB),
    )


def whole(shape):
    return pl.BlockSpec(shape, lambda *_: (0,) * len(shape))


def on_device(grad_terms, error_buffer, weight, q_prev):
    term, error = grad_terms[0, 0], error_buffer[0]
    rows, width = term.shape
    n_rep, n_grp = NY * NC, NZ * NX
    half, cols, slots = rows // 2, width // n_rep, -(-rows // 2 // OWN // n_rep) * OWN
    array = lambda *shape: jax.ShapeDtypeStruct(shape, F32)
    core = lax.axis_index("core")
    place = jnp.stack([lax.axis_index("z") * NX + lax.axis_index("x"), core]).astype(jnp.int32)

    wide, left = call(
        prepare,
        60,
        (2,),
        [
            pl.BlockSpec((half, width), lambda i, _: (i, 0)),
            whole((OWN, width)),
            whole((RANK, width)),
        ],
        [pl.BlockSpec((NX, NZ // 2, OWN, width), lambda i, _: (0, i, 0, 0)), whole((n_rep, slots, LANES))],
        [array(NX, NZ, OWN, width), array(n_rep, slots, LANES)],
        [pltpu.VMEM((3 * RANK, width), BF16), pltpu.VMEM((half, LANES), F32)],
    )(place, term, error, q_prev.T)

    summed_x = scatter(wide.reshape(rows, width), "x")
    summed = scatter(summed_x, "z")

    block = exchange(left, REP).sum(0)
    block = gathered(block, GRP, n_grp).sum(0)
    left = gathered(block, REP, n_rep)

    send, keep, left_own = call(
        right_terms,
        24,
        (4,),
        [
            whole((n_rep, slots, LANES)),
            pl.BlockSpec((rows, width // 4), lambda i, s: (0, (i + 2 - 2 * s[1]) % 4)),
            pl.BlockSpec((OWN, width // 4), lambda i, s: (0, (i + 2 - 2 * s[1]) % 4)),
        ],
        [
            pl.BlockSpec((NY // 2, RANK, cols), lambda i, _: (jnp.minimum(i, 1), 0, 0)),
            pl.BlockSpec((NY // 2, RANK, cols), lambda i, _: (jnp.maximum(i - 2, 0), 0, 0)),
            whole((OWN, RANK)),
        ],
        [array(NY, RANK, cols), array(NY, RANK, cols), array(OWN, RANK)],
        [pltpu.VMEM((half, LANES), F32), pltpu.VMEM((2, 3 * RANK, half), BF16)],
    )(place, left, term, error)
    right = exchange(keep + swap(send), "y")
    used = RANK * cols // LANES
    pieces = -(-used // n_grp)
    flat = pl.pallas_call(
        fold,
        out_shape=array(pieces * n_grp, LANES),
        in_specs=[pl.BlockSpec(memory_space=pltpu.VMEM), pl.BlockSpec(memory_space=pl.ANY)],
        out_specs=pl.BlockSpec(memory_space=pltpu.VMEM),
        compiler_params=pltpu.CompilerParams(vmem_limit_bytes=4 * MIB),
    )(right, summed_x)
    piece = exchange(flat.reshape(n_grp, pieces, LANES), GRP).sum(0)
    flat = gathered(piece, GRP, n_grp).reshape(n_grp * pieces, LANES)
    right = flat[:used].reshape(cols // LANES, RANK, LANES).transpose(1, 0, 2).reshape(RANK, cols)

    both = left.reshape(n_rep * slots, LANES)
    both = full_dot(both.T, both)
    gram = both[:RANK, :RANK] + both[RANK:, RANK:]
    shift = 0.01 * (jnp.trace(gram) / RANK + 1e-06)
    eye = jnp.eye(RANK, dtype=F32)
    lower = jnp.linalg.cholesky(gram + shift * eye)
    inverse = lax.linalg.triangular_solve(lower, eye, left_side=True, lower=True)
    left_hat = full_dot(left_own, inverse.T)

    right = full_dot(inverse, right) / n_rep
    mine = gathered(right, "y", NY)
    other = swap(mine)
    side = pl.BlockSpec((OWN, width // 2), lambda i, _: (0, i))
    q_turned, error_next, weight_next = call(
        finish,
        16,
        (2,),
        [whole((NY, RANK, cols)), whole((NY, RANK, cols)), whole((OWN, RANK)), side, side, side],
        [pl.BlockSpec((RANK, width // 2), lambda i, _: (0, i)), side, side],
        [array(RANK, width), array(OWN, width), array(OWN, width)],
    )(place, mine, other, left_hat, summed, error, weight)
    return (q_turned.T, error_next[None], weight_next)


def solution(mesh):
    split = Mesh(mesh.devices.reshape(NY, NC, NZ, NX), REP + GRP)
    placed = (P(REP, GRP, None, None), P(REP, GRP, None), P(GRP, None), P())
    return jax.shard_map(
        on_device,
        mesh=split,
        in_specs=placed,
        out_specs=(P(), P(REP, GRP, None), P(GRP, None)),
        check_vma=False,
    )
```

```python
import functools

import jax
import jax.numpy as jnp
from jax import lax
from jax.experimental import pallas as pl
from jax.experimental.pallas import tpu as pltpu
from jax.sharding import Mesh, PartitionSpec as P

NY, NC, NZ, NX = 8, 2, 12, 4
REP, GRP = ("y", "core"), ("z", "x")
F32, BF16 = jnp.float32, jnp.bfloat16
RANK, OWN, LANES = 64, 8, 128
HIGHEST = lax.Precision.HIGHEST
MIB = 2**20


def full_dot(left, right):
    return jnp.dot(left, right, precision=HIGHEST)


def parts_of(value):
    high = value.astype(BF16).astype(F32)
    rest = value - high
    middle = rest.astype(BF16).astype(F32)
    return [high, middle, rest - middle]


def stacked(parts):
    return jnp.concatenate(parts, axis=0).astype(BF16)


def dot_nt(left, right):
    return lax.dot_general(left, right, (((1,), (1,)), ((), ())), preferred_element_type=F32)


def exchange(value, axes):
    return lax.all_to_all(value, axes, 0, 0, tiled=True)


def gathered(value, axes, n):
    return exchange(jnp.broadcast_to(value[None], (n,) + value.shape), axes)


def scatter(value, axis):
    return lax.psum_scatter(value, axis, scatter_dimension=0, tiled=True)


def swap(value):
    return lax.ppermute(value, "core", [(i, NC - 1 - i) for i in range(NC)])


def own_place(g, n_tiles):
    low = g < n_tiles
    return low, pl.multiple_of(jnp.where(low, g, g - n_tiles) * OWN, OWN)


def prepare(g_ref, term_ref, error_ref, q_ref, wide_ref, left_ref, parts):
    step = pl.program_id(0)
    rows = term_ref.shape[0]

    @pl.when(step == 0)
    def _():
        for i, part in enumerate(parts_of(q_ref[...])):
            parts[i * RANK : (i + 1) * RANK] = part.astype(BF16)

    block = term_ref[...]
    for z in range(rows // (NX * OWN)):
        band = block[z * NX * OWN : (z + 1) * NX * OWN].astype(F32)
        for x in range(NX):
            wide_ref[x, z] = band[x * OWN : (x + 1) * OWN]
    product = dot_nt(block, parts[...])
    left = product[:, :RANK] + product[:, RANK : 2 * RANK] + product[:, 2 * RANK :]

    @pl.when(step == 0)
    def _():
        left_ref[:, :RANK] = left

    @pl.when(step == 1)
    def _():
        left_ref[:, RANK:] = left
        high, middle, low = parts_of(error_ref[...])
        errors = stacked([high, middle, low, jnp.zeros_like(low)])
        cross = dot_nt(errors, parts[...])
        own = cross[2 * OWN : 3 * OWN, :RANK] + cross[:OWN, 2 * RANK :]
        own = own + cross[OWN : 2 * OWN, RANK : 2 * RANK]
        own = own + cross[OWN : 2 * OWN, :RANK] + cross[:OWN, RANK : 2 * RANK]
        own = own + cross[:OWN, :RANK]
        first, at = own_place(g_ref[0], rows // OWN)
        none = jnp.zeros_like(own)
        pair = jnp.concatenate([jnp.where(first, own, none), jnp.where(first, none, own)], axis=1)
        left_ref[pl.ds(at, OWN), :] += pair


def right_terms(s_ref, left_ref, term_ref, error_ref, send_ref, keep_ref, own_ref, parts):
    step = pl.program_id(0)
    half = term_ref.shape[0] // 2
    first, at = own_place(s_ref[0], half // OWN)

    @pl.when(step == 0)
    def _():
        turned = left_ref[...].T
        for i in range(2):
            for j, part in enumerate(parts_of(turned[i * RANK : (i + 1) * RANK])):
                parts[i, j * RANK : (j + 1) * RANK] = part.astype(BF16)
        pair = left_ref[pl.ds(at, OWN), :]
        own_ref[...] = jnp.where(first, pair[:, :RANK], pair[:, RANK:])

    total = jnp.dot(parts[0], term_ref[:half], preferred_element_type=F32)
    total = total + jnp.dot(parts[1], term_ref[half:], preferred_element_type=F32)
    total = total[:RANK] + total[RANK : 2 * RANK] + total[2 * RANK :]
    total = total + lax.dot_general(
        own_ref[...], error_ref[...], (((0,), (0,)), ((), ())), precision=HIGHEST, preferred_element_type=F32
    )
    count, cols = send_ref.shape[0], send_ref.shape[2]

    @pl.when(step < 2)
    def _():
        for k in range(count):
            send_ref[k] = total[:, k * cols : (k + 1) * cols]

    @pl.when(step >= 2)
    def _():
        for k in range(count):
            keep_ref[k] = total[:, k * cols : (k + 1) * cols]


def fold(blocks_ref, _, total_ref, __):
    total = blocks_ref[0]
    for i in range(1, blocks_ref.shape[0]):
        total = total + blocks_ref[i]
    total_ref[...] = total


def finish(s_ref, mine_ref, other_ref, inverse_ref, left_ref, summed_ref, error_ref, weight_ref, q_ref, error_out, weight_out):
    step = pl.program_id(0)
    cols = mine_ref.shape[2]

    def run(blocks_ref):
        for k in range(blocks_ref.shape[0]):
            at = slice(k * cols, (k + 1) * cols)
            block = jnp.dot(inverse_ref[...], blocks_ref[k], precision=HIGHEST, preferred_element_type=F32)
            q_ref[:, at] = block
            approx = jnp.dot(left_ref[...], block, precision=HIGHEST, preferred_element_type=F32)
            error_out[:, at] = summed_ref[:, at] + error_ref[:, at] - approx
            weight_out[:, at] = weight_ref[:, at] - 0.5 * approx

    pl.when(step == s_ref[1])(functools.partial(run, mine_ref))
    pl.when(step != s_ref[1])(functools.partial(run, other_ref))


def call(kernel, room, grid, in_specs, out_specs, out_shape, scratch=()):
    return pl.pallas_call(
        kernel,
        out_shape=out_shape,
        grid_spec=pltpu.PrefetchScalarGridSpec(
            num_scalar_prefetch=1, grid=grid, in_specs=in_specs, out_specs=out_specs, scratch_shapes=list(scratch)
        ),
        compiler_params=pltpu.CompilerParams(vmem_limit_bytes=room * MIB),
    )


def whole(shape):
    return pl.BlockSpec(shape, lambda *_: (0,) * len(shape))


def on_device(grad_terms, error_buffer, weight, q_prev):
    term, error = grad_terms[0, 0], error_buffer[0]
    rows, width = term.shape
    half, cols = rows // 2, width // (NY * NC)
    array = lambda *shape: jax.ShapeDtypeStruct(shape, F32)
    core = lax.axis_index("core")
    place = jnp.stack([lax.axis_index("z") * NX + lax.axis_index("x"), core]).astype(jnp.int32)

    wide, left = call(
        prepare,
        60,
        (2,),
        [
            pl.BlockSpec((half, width), lambda i, _: (i, 0)),
            whole((OWN, width)),
            whole((RANK, width)),
        ],
        [pl.BlockSpec((NX, NZ // 2, OWN, width), lambda i, _: (0, i, 0, 0)), whole((half, LANES))],
        [array(NX, NZ, OWN, width), array(half, LANES)],
        [pltpu.VMEM((3 * RANK, width), BF16)],
    )(place, term, error, q_prev.T)

    tile = exchange(left.reshape(NZ * NC, half // (NZ * NC), LANES), ("z", "core")).sum(0)
    tile = gathered(tile, ("y", "x"), NY * NX).sum(0)
    left = gathered(tile, ("z", "core"), NZ * NC).reshape(half, LANES)

    send, keep, left_own = call(
        right_terms,
        24,
        (4,),
        [
            whole((half, LANES)),
            pl.BlockSpec((rows, width // 4), lambda i, s: (0, (i + 2 - 2 * s[1]) % 4)),
            pl.BlockSpec((OWN, width // 4), lambda i, s: (0, (i + 2 - 2 * s[1]) % 4)),
        ],
        [
            pl.BlockSpec((NY // 2, RANK, cols), lambda i, _: (jnp.minimum(i, 1), 0, 0)),
            pl.BlockSpec((NY // 2, RANK, cols), lambda i, _: (jnp.maximum(i - 2, 0), 0, 0)),
            whole((OWN, RANK)),
        ],
        [array(NY, RANK, cols), array(NY, RANK, cols), array(OWN, RANK)],
        [pltpu.VMEM((2, 3 * RANK, half), BF16)],
    )(place, left, term, error)
    blocks = exchange((keep + swap(send)).reshape(NY * NX, RANK // NX, cols), ("y", "x"))

    summed = scatter(wide.reshape(rows, width), "x")
    vmem, anywhere = pl.BlockSpec(memory_space=pltpu.VMEM), pl.BlockSpec(memory_space=pl.ANY)
    block, summed = pl.pallas_call(
        fold,
        out_shape=(array(RANK // NX, cols), array(*summed.shape)),
        in_specs=[vmem, anywhere],
        out_specs=(vmem, anywhere),
        input_output_aliases={1: 1},
        compiler_params=pltpu.CompilerParams(vmem_limit_bytes=60 * MIB),
    )(blocks, summed)
    summed = scatter(summed, "z")

    block = gathered(block, "z", NZ).sum(0)
    mine = gathered(block, ("y", "x"), NY * NX).reshape(NY, RANK, cols)
    other = swap(mine)

    both = full_dot(left.T, left)
    gram = both[:RANK, :RANK] + both[RANK:, RANK:]
    shift = 0.01 * (jnp.trace(gram) / RANK + 1e-06)
    eye = jnp.eye(RANK, dtype=F32)
    lower = jnp.linalg.cholesky(gram + shift * eye)
    inverse = lax.linalg.triangular_solve(lower, eye, left_side=True, lower=True)
    left_hat = full_dot(left_own, inverse.T)

    side = pl.BlockSpec((OWN, width // 2), lambda i, _: (0, i))
    q_turned, error_next, weight_next = call(
        finish,
        16,
        (2,),
        [whole((NY, RANK, cols)), whole((NY, RANK, cols)), whole((RANK, RANK)), whole((OWN, RANK)), side, side, side],
        [pl.BlockSpec((RANK, width // 2), lambda i, _: (0, i)), side, side],
        [array(RANK, width), array(OWN, width), array(OWN, width)],
    )(place, mine, other, inverse / (NY * NC), left_hat, summed, error, weight)
    return (q_turned.T, error_next[None], weight_next)


def solution(mesh):
    split = Mesh(mesh.devices.reshape(NY, NC, NZ, NX), REP + GRP)
    placed = (P(REP, GRP, None, None), P(REP, GRP, None), P(GRP, None), P())
    return jax.shard_map(
        on_device,
        mesh=split,
        in_specs=placed,
        out_specs=(P(), P(REP, GRP, None), P(GRP, None)),
        check_vma=False,
    )
```

```python
import functools

import jax
import jax.numpy as jnp
from jax import lax
from jax.experimental import pallas as pl
from jax.experimental.pallas import tpu as pltpu
from jax.sharding import Mesh, PartitionSpec as P

NY, NC, NZ, NX = 8, 2, 12, 4
REP, GRP = ("y", "core"), ("z", "x")
F32, BF16 = jnp.float32, jnp.bfloat16
RANK, OWN, LANES = 64, 8, 128
HIGHEST = lax.Precision.HIGHEST
MIB = 2**20


def parts_of(value):
    high = value.astype(BF16).astype(F32)
    rest = value - high
    middle = rest.astype(BF16).astype(F32)
    return [high, middle, rest - middle]


def stacked(parts):
    return jnp.concatenate(parts, axis=0).astype(BF16)


def dot_nt(left, right):
    return lax.dot_general(left, right, (((1,), (1,)), ((), ())), preferred_element_type=F32)


def exchange(value, axes):
    return lax.all_to_all(value, axes, 0, 0, tiled=True)


def gathered(value, axes, n):
    return exchange(jnp.broadcast_to(value[None], (n,) + value.shape), axes)


def scatter(value, axis):
    return lax.psum_scatter(value, axis, scatter_dimension=0, tiled=True)


def swap(value):
    return lax.ppermute(value, "core", [(i, NC - 1 - i) for i in range(NC)])


def own_place(g, n_tiles):
    low = g < n_tiles
    return low, pl.multiple_of(jnp.where(low, g, g - n_tiles) * OWN, OWN)


def prepare(g_ref, term_ref, error_ref, q_ref, wide_ref, left_ref, parts):
    step = pl.program_id(0)
    rows = term_ref.shape[0]

    @pl.when(step == 0)
    def _():
        for i, part in enumerate(parts_of(q_ref[...])):
            parts[i * RANK : (i + 1) * RANK] = part.astype(BF16)

    block = term_ref[...]
    for z in range(rows // (NX * OWN)):
        band = block[z * NX * OWN : (z + 1) * NX * OWN].astype(F32)
        for x in range(NX):
            wide_ref[x, z] = band[x * OWN : (x + 1) * OWN]
    product = dot_nt(block, parts[...])
    left = product[:, :RANK] + product[:, RANK : 2 * RANK] + product[:, 2 * RANK :]

    @pl.when(step == 0)
    def _():
        left_ref[:, :RANK] = left

    @pl.when(step == 1)
    def _():
        left_ref[:, RANK:] = left
        high, middle, low = parts_of(error_ref[...])
        errors = stacked([high, middle, low, jnp.zeros_like(low)])
        cross = dot_nt(errors, parts[...])
        own = cross[2 * OWN : 3 * OWN, :RANK] + cross[:OWN, 2 * RANK :]
        own = own + cross[OWN : 2 * OWN, RANK : 2 * RANK]
        own = own + cross[OWN : 2 * OWN, :RANK] + cross[:OWN, RANK : 2 * RANK]
        own = own + cross[:OWN, :RANK]
        first, at = own_place(g_ref[0], rows // OWN)
        none = jnp.zeros_like(own)
        pair = jnp.concatenate([jnp.where(first, own, none), jnp.where(first, none, own)], axis=1)
        left_ref[pl.ds(at, OWN), :] += pair


def right_terms(s_ref, left_ref, term_ref, error_ref, send_ref, keep_ref, own_ref, parts):
    step = pl.program_id(0)
    half = term_ref.shape[0] // 2
    first, at = own_place(s_ref[0], half // OWN)

    @pl.when(step == 0)
    def _():
        turned = left_ref[...].T
        for i in range(2):
            for j, part in enumerate(parts_of(turned[i * RANK : (i + 1) * RANK])):
                parts[i, j * RANK : (j + 1) * RANK] = part.astype(BF16)
        pair = left_ref[pl.ds(at, OWN), :]
        own_ref[...] = jnp.where(first, pair[:, :RANK], pair[:, RANK:])

    total = jnp.dot(parts[0], term_ref[:half], preferred_element_type=F32)
    total = total + jnp.dot(parts[1], term_ref[half:], preferred_element_type=F32)
    total = total[:RANK] + total[RANK : 2 * RANK] + total[2 * RANK :]
    total = total + lax.dot_general(
        own_ref[...], error_ref[...], (((0,), (0,)), ((), ())), precision=HIGHEST, preferred_element_type=F32
    )
    count, cols = send_ref.shape[0], send_ref.shape[2]

    @pl.when(step < 2)
    def _():
        for k in range(count):
            send_ref[k] = total[:, k * cols : (k + 1) * cols]

    @pl.when(step >= 2)
    def _():
        for k in range(count):
            keep_ref[k] = total[:, k * cols : (k + 1) * cols]


def hand_on(_, __, ___):
    pass


def products(left, right):
    a, b = parts_of(left), parts_of(right)
    order = ((0, 0), (0, 1), (1, 0), (1, 1), (0, 2), (2, 0))
    wide = jnp.concatenate([a[i] for i, _ in order], axis=1).astype(BF16)
    return jnp.dot(wide, stacked([b[j] for _, j in order]), preferred_element_type=F32)


def triangle(left_ref, own_ref, inverse_ref, hat_ref):
    packed = left_ref[...]
    both = products(packed.T, packed)
    gram = both[:RANK, :RANK] + both[RANK:, RANK:]
    row = lax.broadcasted_iota(jnp.int32, (RANK, RANK), 0)
    diagonal = row == lax.broadcasted_iota(jnp.int32, (RANK, RANK), 1)
    shift = 0.01 * (jnp.sum(jnp.where(diagonal, gram, 0.0)) / RANK + 1e-06)
    eye = jnp.where(diagonal, 1.0, 0.0)
    work = jnp.concatenate([gram + shift * eye, eye], axis=1)
    below = lax.broadcasted_iota(jnp.int32, (RANK, 1), 0)
    scale = jnp.zeros((RANK, 1), F32)
    for k in range(RANK):
        column, line = work[:, k : k + 1], work[k : k + 1]
        pivot = line[:, k : k + 1]
        scale = jnp.where(below == k, pivot, scale)
        work = work - jnp.where(below > k, column / pivot, 0.0) * line
    inverse = work[:, RANK:] * lax.rsqrt(scale)
    inverse_ref[...] = inverse / (NY * NC)
    hat_ref[...] = lax.dot_general(
        own_ref[...], inverse, (((1,), (1,)), ((), ())), precision=HIGHEST, preferred_element_type=F32
    )


def apply(blocks_ref, inverse_ref, q_ref):
    for k in range(blocks_ref.shape[0]):
        q_ref[k] = products(inverse_ref[...], blocks_ref[k])


def finish(s_ref, mine_ref, other_ref, left_ref, weight_ref, q_ref, approx_out, weight_out):
    step = pl.program_id(0)
    cols = mine_ref.shape[2]

    def run(blocks_ref):
        for k in range(blocks_ref.shape[0]):
            at = slice(k * cols, (k + 1) * cols)
            block = blocks_ref[k]
            q_ref[:, at] = block
            approx = products(left_ref[...], block)
            approx_out[:, at] = approx
            weight_out[:, at] = weight_ref[:, at] - 0.5 * approx

    pl.when(step == s_ref[1])(functools.partial(run, mine_ref))
    pl.when(step != s_ref[1])(functools.partial(run, other_ref))


def call(kernel, room, grid, in_specs, out_specs, out_shape, scratch=()):
    return pl.pallas_call(
        kernel,
        out_shape=out_shape,
        grid_spec=pltpu.PrefetchScalarGridSpec(
            num_scalar_prefetch=1, grid=grid, in_specs=in_specs, out_specs=out_specs, scratch_shapes=list(scratch)
        ),
        compiler_params=pltpu.CompilerParams(vmem_limit_bytes=room * MIB),
    )


def whole(shape):
    return pl.BlockSpec(shape, lambda *_: (0,) * len(shape))


def on_device(grad_terms, error_buffer, weight, q_prev):
    term, error = grad_terms[0, 0], error_buffer[0]
    rows, width = term.shape
    half, cols = rows // 2, width // (NY * NC)
    array = lambda *shape: jax.ShapeDtypeStruct(shape, F32)
    core = lax.axis_index("core")
    place = jnp.stack([lax.axis_index("z") * NX + lax.axis_index("x"), core]).astype(jnp.int32)

    wide, left = call(
        prepare,
        60,
        (2,),
        [
            pl.BlockSpec((half, width), lambda i, _: (i, 0)),
            whole((OWN, width)),
            whole((RANK, width)),
        ],
        [pl.BlockSpec((NX, NZ // 2, OWN, width), lambda i, _: (0, i, 0, 0)), whole((half, LANES))],
        [array(NX, NZ, OWN, width), array(half, LANES)],
        [pltpu.VMEM((3 * RANK, width), BF16)],
    )(place, term, error, q_prev.T)

    tile = exchange(left.reshape(NZ * NC, half // (NZ * NC), LANES), ("z", "core")).sum(0)
    tile = gathered(tile, ("y", "x"), NY * NX).sum(0)
    left = gathered(tile, ("z", "core"), NZ * NC).reshape(half, LANES)

    send, keep, left_own = call(
        right_terms,
        24,
        (4,),
        [
            whole((half, LANES)),
            pl.BlockSpec((rows, width // 4), lambda i, s: (0, (i + 2 - 2 * s[1]) % 4)),
            pl.BlockSpec((OWN, width // 4), lambda i, s: (0, (i + 2 - 2 * s[1]) % 4)),
        ],
        [
            pl.BlockSpec((NY // 2, RANK, cols), lambda i, _: (jnp.minimum(i, 1), 0, 0)),
            pl.BlockSpec((NY // 2, RANK, cols), lambda i, _: (jnp.maximum(i - 2, 0), 0, 0)),
            whole((OWN, RANK)),
        ],
        [array(NY, RANK, cols), array(NY, RANK, cols), array(OWN, RANK)],
        [pltpu.VMEM((2, 3 * RANK, half), BF16)],
    )(place, left, term, error)
    half_sum = keep + swap(send)

    inverse, left_hat = pl.pallas_call(
        triangle,
        out_shape=(array(RANK, RANK), array(OWN, RANK)),
        compiler_params=pltpu.CompilerParams(vmem_limit_bytes=8 * MIB),
        cost_estimate=pl.CostEstimate(flops=20 * 10**9, bytes_accessed=4 * half * LANES, transcendentals=RANK),
    )(left, left_own)

    summed = scatter(wide.reshape(rows, width), "x")
    anywhere = pl.BlockSpec(memory_space=pl.ANY)
    summed = pl.pallas_call(
        hand_on,
        out_shape=array(*summed.shape),
        in_specs=[anywhere, anywhere],
        out_specs=anywhere,
        input_output_aliases={1: 0},
        compiler_params=pltpu.CompilerParams(vmem_limit_bytes=60 * MIB),
    )(half_sum, summed)
    summed = scatter(summed, "z")

    block = exchange(half_sum.reshape(NY * NX, RANK // NX, cols), ("y", "x")).sum(0)
    block = gathered(block, "z", NZ).sum(0)
    mine = pl.pallas_call(
        apply,
        out_shape=array(NY, RANK, cols),
        compiler_params=pltpu.CompilerParams(vmem_limit_bytes=8 * MIB),
    )(gathered(block, ("y", "x"), NY * NX).reshape(NY, RANK, cols), inverse)
    other = swap(mine)
    side = pl.BlockSpec((OWN, width // 2), lambda i, _: (0, i))
    q_turned, approx, weight_next = call(
        finish,
        16,
        (2,),
        [whole((NY, RANK, cols)), whole((NY, RANK, cols)), whole((OWN, RANK)), side],
        [pl.BlockSpec((RANK, width // 2), lambda i, _: (0, i)), side, side],
        [array(RANK, width), array(OWN, width), array(OWN, width)],
    )(place, mine, other, left_hat, weight)
    return (q_turned.T, (summed + error - approx)[None], weight_next)


def solution(mesh):
    split = Mesh(mesh.devices.reshape(NY, NC, NZ, NX), REP + GRP)
    placed = (P(REP, GRP, None, None), P(REP, GRP, None), P(GRP, None), P())
    return jax.shard_map(
        on_device,
        mesh=split,
        in_specs=placed,
        out_specs=(P(), P(REP, GRP, None), P(GRP, None)),
        check_vma=False,
    )
```

```python
import functools

import jax
import jax.numpy as jnp
from jax import lax
from jax.experimental import pallas as pl
from jax.experimental.pallas import tpu as pltpu
from jax.sharding import Mesh, PartitionSpec as P

NY, NC, NZ, NX = 8, 2, 12, 4
REP, GRP = ("y", "core"), ("z", "x")
F32, BF16 = jnp.float32, jnp.bfloat16
RANK, OWN, LANES = 64, 8, 128
HIGHEST = lax.Precision.HIGHEST
MIB = 2**20
PAIRS = ((0, 0), (0, 1), (1, 0), (1, 1), (0, 2), (2, 0))


def parts_of(value):
    high = value.astype(BF16).astype(F32)
    rest = value - high
    middle = rest.astype(BF16).astype(F32)
    return [high, middle, rest - middle]


def stacked(parts):
    return jnp.concatenate(parts, axis=0).astype(BF16)


def dot_nt(left, right):
    return lax.dot_general(left, right, (((1,), (1,)), ((), ())), preferred_element_type=F32)


def exchange(value, axes):
    return lax.all_to_all(value, axes, 0, 0, tiled=True)


def gathered(value, axes, n):
    return exchange(jnp.broadcast_to(value[None], (n,) + value.shape), axes)


def scatter(value, axis):
    return lax.psum_scatter(value, axis, scatter_dimension=0, tiled=True)


def swap(value):
    return lax.ppermute(value, "core", [(i, NC - 1 - i) for i in range(NC)])


def own_place(g, n_tiles):
    low = g < n_tiles
    return low, pl.multiple_of(jnp.where(low, g, g - n_tiles) * OWN, OWN)


def widen(term_ref, wide_ref):
    block = term_ref[...].astype(F32)
    for z in range(wide_ref.shape[1]):
        for x in range(NX):
            at = (z * NX + x) * OWN
            wide_ref[x, z] = block[at : at + OWN]


def left_terms(term_ref, error_ref, q_ref, left_ref, parts):
    step = pl.program_id(0)
    rows = term_ref.shape[0]

    @pl.when(step == 0)
    def _():
        for i, part in enumerate(parts_of(q_ref[...])):
            parts[i * RANK : (i + 1) * RANK] = part.astype(BF16)

    product = dot_nt(term_ref[...], parts[...])
    left = product[:, :RANK] + product[:, RANK : 2 * RANK] + product[:, 2 * RANK :]

    @pl.when(step == 0)
    def _():
        left_ref[:, :RANK] = left

    @pl.when(step == 1)
    def _():
        left_ref[:, RANK:] = left
        high, middle, low = parts_of(error_ref[...])
        errors = stacked([high, middle, low, jnp.zeros_like(low)])
        cross = dot_nt(errors, parts[...])
        own = cross[2 * OWN : 3 * OWN, :RANK] + cross[:OWN, 2 * RANK :]
        own = own + cross[OWN : 2 * OWN, RANK : 2 * RANK]
        own = own + cross[OWN : 2 * OWN, :RANK] + cross[:OWN, RANK : 2 * RANK]
        own = own + cross[:OWN, :RANK]
        first, at = own_place(lax.axis_index("z") * NX + lax.axis_index("x"), rows // OWN)
        none = jnp.zeros_like(own)
        pair = jnp.concatenate([jnp.where(first, own, none), jnp.where(first, none, own)], axis=1)
        left_ref[pl.ds(at, OWN), :] += pair


def right_terms(s_ref, left_ref, term_ref, error_ref, send_ref, keep_ref, own_ref, parts, own_parts):
    step = pl.program_id(0)
    half = term_ref.shape[0] // 2
    first, at = own_place(s_ref[0], half // OWN)

    @pl.when(step == 0)
    def _():
        turned = left_ref[...].T
        for i in range(2):
            for j, part in enumerate(parts_of(turned[i * RANK : (i + 1) * RANK])):
                parts[i, j * RANK : (j + 1) * RANK] = part.astype(BF16)
        pair = left_ref[pl.ds(at, OWN), :]
        own = jnp.where(first, pair[:, :RANK], pair[:, RANK:])
        own_ref[...] = own
        cut = parts_of(own)
        own_parts[...] = jnp.concatenate([cut[i] for i, _ in PAIRS], axis=0).T.astype(BF16)

    total = jnp.dot(parts[0], term_ref[:half], preferred_element_type=F32)
    total = total + jnp.dot(parts[1], term_ref[half:], preferred_element_type=F32)
    total = total[:RANK] + total[RANK : 2 * RANK] + total[2 * RANK :]
    cut = parts_of(error_ref[...])
    total = total + jnp.dot(own_parts[...], stacked([cut[j] for _, j in PAIRS]), preferred_element_type=F32)
    count, cols = send_ref.shape[0], send_ref.shape[2]

    @pl.when(step < 2)
    def _():
        for k in range(count):
            send_ref[k] = total[:, k * cols : (k + 1) * cols]

    @pl.when(step >= 2)
    def _():
        for k in range(count):
            keep_ref[k] = total[:, k * cols : (k + 1) * cols]


def hand_on(_, __, ___):
    pass


def products(left, right):
    a, b = parts_of(left), parts_of(right)
    wide = jnp.concatenate([a[i] for i, _ in PAIRS], axis=1).astype(BF16)
    return jnp.dot(wide, stacked([b[j] for _, j in PAIRS]), preferred_element_type=F32)


def triangle(left_ref, own_ref, inverse_ref, hat_ref):
    packed = left_ref[...]
    both = products(packed.T, packed)
    gram = both[:RANK, :RANK] + both[RANK:, RANK:]
    row = lax.broadcasted_iota(jnp.int32, (RANK, RANK), 0)
    diagonal = row == lax.broadcasted_iota(jnp.int32, (RANK, RANK), 1)
    shift = 0.01 * (jnp.sum(jnp.where(diagonal, gram, 0.0)) / RANK + 1e-06)
    eye = jnp.where(diagonal, 1.0, 0.0)
    work = jnp.concatenate([gram + shift * eye, eye], axis=1)
    below = lax.broadcasted_iota(jnp.int32, (RANK, 1), 0)
    scale = jnp.zeros((RANK, 1), F32)
    for k in range(RANK):
        column, line = work[:, k : k + 1], work[k : k + 1]
        pivot = line[:, k : k + 1]
        scale = jnp.where(below == k, pivot, scale)
        work = work - jnp.where(below > k, column / pivot, 0.0) * line
    inverse = work[:, RANK:] * lax.rsqrt(scale)
    inverse_ref[...] = inverse / (NY * NC)
    hat_ref[...] = lax.dot_general(
        own_ref[...], inverse, (((1,), (1,)), ((), ())), precision=HIGHEST, preferred_element_type=F32
    )


def apply(blocks_ref, inverse_ref, q_ref):
    for k in range(blocks_ref.shape[0]):
        q_ref[k] = products(inverse_ref[...], blocks_ref[k])


def finish(s_ref, mine_ref, other_ref, left_ref, weight_ref, q_ref, approx_out, weight_out):
    step = pl.program_id(0)
    cols = mine_ref.shape[2]

    def run(blocks_ref):
        for k in range(blocks_ref.shape[0]):
            at = slice(k * cols, (k + 1) * cols)
            block = blocks_ref[k]
            q_ref[:, at] = block
            approx = products(left_ref[...], block)
            approx_out[:, at] = approx
            weight_out[:, at] = weight_ref[:, at] - 0.5 * approx

    pl.when(step == s_ref[1])(functools.partial(run, mine_ref))
    pl.when(step != s_ref[1])(functools.partial(run, other_ref))


def call(kernel, room, grid, in_specs, out_specs, out_shape, scratch=()):
    return pl.pallas_call(
        kernel,
        out_shape=out_shape,
        grid_spec=pltpu.PrefetchScalarGridSpec(
            num_scalar_prefetch=1, grid=grid, in_specs=in_specs, out_specs=out_specs, scratch_shapes=list(scratch)
        ),
        compiler_params=pltpu.CompilerParams(vmem_limit_bytes=room * MIB),
    )


def whole(shape):
    return pl.BlockSpec(shape, lambda *_: (0,) * len(shape))


def on_device(grad_terms, error_buffer, weight, q_prev):
    term, error = grad_terms[0, 0], error_buffer[0]
    rows, width = term.shape
    half, cols = rows // 2, width // (NY * NC)
    array = lambda *shape: jax.ShapeDtypeStruct(shape, F32)
    core = lax.axis_index("core")
    place = jnp.stack([lax.axis_index("z") * NX + lax.axis_index("x"), core]).astype(jnp.int32)

    wide = pl.pallas_call(
        widen,
        out_shape=array(NX, NZ, OWN, width),
        grid=(NZ // 2,),
        in_specs=[pl.BlockSpec((2 * NX * OWN, width), lambda i: (i, 0))],
        out_specs=pl.BlockSpec((NX, 2, OWN, width), lambda i: (0, i, 0, 0)),
        compiler_params=pltpu.CompilerParams(vmem_limit_bytes=60 * MIB),
    )(term)
    left = pl.pallas_call(
        left_terms,
        out_shape=array(half, LANES),
        grid=(2,),
        in_specs=[pl.BlockSpec((half, width), lambda i: (i, 0)), whole((OWN, width)), whole((RANK, width))],
        out_specs=whole((half, LANES)),
        scratch_shapes=[pltpu.VMEM((3 * RANK, width), BF16)],
        compiler_params=pltpu.CompilerParams(vmem_limit_bytes=60 * MIB),
    )(term, error, q_prev.T)

    tile = exchange(left.reshape(NZ * NC, half // (NZ * NC), LANES), ("z", "core")).sum(0)
    tile = gathered(tile, ("y", "x"), NY * NX).sum(0)
    left = gathered(tile, ("z", "core"), NZ * NC).reshape(half, LANES)

    send, keep, left_own = call(
        right_terms,
        24,
        (4,),
        [
            whole((half, LANES)),
            pl.BlockSpec((rows, width // 4), lambda i, s: (0, (i + 2 - 2 * s[1]) % 4)),
            pl.BlockSpec((OWN, width // 4), lambda i, s: (0, (i + 2 - 2 * s[1]) % 4)),
        ],
        [
            pl.BlockSpec((NY // 2, RANK, cols), lambda i, _: (jnp.minimum(i, 1), 0, 0)),
            pl.BlockSpec((NY // 2, RANK, cols), lambda i, _: (jnp.maximum(i - 2, 0), 0, 0)),
            whole((OWN, RANK)),
        ],
        [array(NY, RANK, cols), array(NY, RANK, cols), array(OWN, RANK)],
        [pltpu.VMEM((2, 3 * RANK, half), BF16), pltpu.VMEM((RANK, len(PAIRS) * OWN), BF16)],
    )(place, left, term, error)
    half_sum = keep + swap(send)

    inverse, left_hat = pl.pallas_call(
        triangle,
        out_shape=(array(RANK, RANK), array(OWN, RANK)),
        compiler_params=pltpu.CompilerParams(vmem_limit_bytes=8 * MIB),
        cost_estimate=pl.CostEstimate(flops=20 * 10**9, bytes_accessed=4 * half * LANES, transcendentals=RANK),
    )(left, left_own)

    summed = scatter(wide.reshape(rows, width), "x")
    anywhere = pl.BlockSpec(memory_space=pl.ANY)
    summed = pl.pallas_call(
        hand_on,
        out_shape=array(*summed.shape),
        in_specs=[anywhere, anywhere],
        out_specs=anywhere,
        input_output_aliases={1: 0},
        compiler_params=pltpu.CompilerParams(vmem_limit_bytes=60 * MIB),
    )(half_sum, summed)
    summed = scatter(summed, "z")

    block = exchange(half_sum.reshape(NY * NX, RANK // NX, cols), ("y", "x")).sum(0)
    block = gathered(block, "z", NZ).sum(0)
    mine = pl.pallas_call(
        apply,
        out_shape=array(NY, RANK, cols),
        compiler_params=pltpu.CompilerParams(vmem_limit_bytes=8 * MIB),
    )(gathered(block, ("y", "x"), NY * NX).reshape(NY, RANK, cols), inverse)
    other = swap(mine)
    side = pl.BlockSpec((OWN, width // 2), lambda i, _: (0, i))
    q_turned, approx, weight_next = call(
        finish,
        16,
        (2,),
        [whole((NY, RANK, cols)), whole((NY, RANK, cols)), whole((OWN, RANK)), side],
        [pl.BlockSpec((RANK, width // 2), lambda i, _: (0, i)), side, side],
        [array(RANK, width), array(OWN, width), array(OWN, width)],
    )(place, mine, other, left_hat, weight)
    return (q_turned.T, (summed + error - approx)[None], weight_next)


def solution(mesh):
    split = Mesh(mesh.devices.reshape(NY, NC, NZ, NX), REP + GRP)
    placed = (P(REP, GRP, None, None), P(REP, GRP, None), P(GRP, None), P())
    return jax.shard_map(
        on_device,
        mesh=split,
        in_specs=placed,
        out_specs=(P(), P(REP, GRP, None), P(GRP, None)),
        check_vma=False,
    )
```

```python
import functools

import jax
import jax.numpy as jnp
from jax import lax
from jax.experimental import pallas as pl
from jax.experimental.pallas import tpu as pltpu
from jax.sharding import Mesh, PartitionSpec as P

NY, NC, NZ, NX = 8, 2, 12, 4
REP, GRP = ("y", "core"), ("z", "x")
F32, BF16 = jnp.float32, jnp.bfloat16
RANK, OWN, LANES = 64, 8, 128
HIGHEST = lax.Precision.HIGHEST
MIB = 2**20
PAIRS = ((0, 0), (0, 1), (1, 0), (1, 1), (0, 2), (2, 0))


def parts_of(value):
    high = value.astype(BF16).astype(F32)
    rest = value - high
    middle = rest.astype(BF16).astype(F32)
    return [high, middle, rest - middle]


def stacked(parts):
    return jnp.concatenate(parts, axis=0).astype(BF16)


def dot_nt(left, right):
    return lax.dot_general(left, right, (((1,), (1,)), ((), ())), preferred_element_type=F32)


def exchange(value, axes):
    return lax.all_to_all(value, axes, 0, 0, tiled=True)


def gathered(value, axes, n):
    return exchange(jnp.broadcast_to(value[None], (n,) + value.shape), axes)


def scatter(value, axis):
    return lax.psum_scatter(value, axis, scatter_dimension=0, tiled=True)


def swap(value):
    return lax.ppermute(value, "core", [(i, NC - 1 - i) for i in range(NC)])


def own_place(g, n_tiles):
    low = g < n_tiles
    return low, pl.multiple_of(jnp.where(low, g, g - n_tiles) * OWN, OWN)


def widen(term_ref, wide_ref, narrow, wide, arrived, left):
    bands = narrow.shape[0]
    per = NZ // bands
    size = per * NX * OWN
    reads = [pltpu.make_async_copy(term_ref.at[pl.ds(i * size, size)], narrow.at[i], arrived.at[i]) for i in range(bands)]
    writes = [pltpu.make_async_copy(wide.at[i], wide_ref.at[:, pl.ds(i * per, per)], left.at[i]) for i in range(bands)]
    for copy in reads:
        copy.start()
    for i in range(bands):
        reads[i].wait()
        block = narrow[i].astype(F32)
        for z in range(per):
            for x in range(NX):
                at = (z * NX + x) * OWN
                wide[i, x, z] = block[at : at + OWN]
        writes[i].start()
    for copy in writes:
        copy.wait()


def left_terms(term_ref, error_ref, q_ref, left_ref, parts):
    step = pl.program_id(0)
    rows = term_ref.shape[0]

    @pl.when(step == 0)
    def _():
        for i, part in enumerate(parts_of(q_ref[...])):
            parts[i * RANK : (i + 1) * RANK] = part.astype(BF16)

    product = dot_nt(term_ref[...], parts[...])
    left = product[:, :RANK] + product[:, RANK : 2 * RANK] + product[:, 2 * RANK :]

    @pl.when(step == 0)
    def _():
        left_ref[:, :RANK] = left

    @pl.when(step == 1)
    def _():
        left_ref[:, RANK:] = left
        high, middle, low = parts_of(error_ref[...])
        errors = stacked([high, middle, low, jnp.zeros_like(low)])
        cross = dot_nt(errors, parts[...])
        own = cross[2 * OWN : 3 * OWN, :RANK] + cross[:OWN, 2 * RANK :]
        own = own + cross[OWN : 2 * OWN, RANK : 2 * RANK]
        own = own + cross[OWN : 2 * OWN, :RANK] + cross[:OWN, RANK : 2 * RANK]
        own = own + cross[:OWN, :RANK]
        first, at = own_place(lax.axis_index("z") * NX + lax.axis_index("x"), rows // OWN)
        none = jnp.zeros_like(own)
        pair = jnp.concatenate([jnp.where(first, own, none), jnp.where(first, none, own)], axis=1)
        left_ref[pl.ds(at, OWN), :] += pair


def right_terms(s_ref, left_ref, term_ref, error_ref, send_ref, keep_ref, own_ref, parts, own_parts):
    step = pl.program_id(0)
    half = term_ref.shape[0] // 2
    first, at = own_place(s_ref[0], half // OWN)

    @pl.when(step == 0)
    def _():
        turned = left_ref[...].T
        for i in range(2):
            for j, part in enumerate(parts_of(turned[i * RANK : (i + 1) * RANK])):
                parts[i, j * RANK : (j + 1) * RANK] = part.astype(BF16)
        pair = left_ref[pl.ds(at, OWN), :]
        own = jnp.where(first, pair[:, :RANK], pair[:, RANK:])
        own_ref[...] = own
        cut = parts_of(own)
        own_parts[...] = jnp.concatenate([cut[i] for i, _ in PAIRS], axis=0).T.astype(BF16)

    total = jnp.dot(parts[0], term_ref[:half], preferred_element_type=F32)
    total = total + jnp.dot(parts[1], term_ref[half:], preferred_element_type=F32)
    total = total[:RANK] + total[RANK : 2 * RANK] + total[2 * RANK :]
    cut = parts_of(error_ref[...])
    total = total + jnp.dot(own_parts[...], stacked([cut[j] for _, j in PAIRS]), preferred_element_type=F32)
    count, cols = send_ref.shape[0], send_ref.shape[2]

    @pl.when(step < 2)
    def _():
        for k in range(count):
            send_ref[k] = total[:, k * cols : (k + 1) * cols]

    @pl.when(step >= 2)
    def _():
        for k in range(count):
            keep_ref[k] = total[:, k * cols : (k + 1) * cols]


def hand_on(_, __, ___):
    pass


def products(left, right):
    a, b = parts_of(left), parts_of(right)
    wide = jnp.concatenate([a[i] for i, _ in PAIRS], axis=1).astype(BF16)
    return jnp.dot(wide, stacked([b[j] for _, j in PAIRS]), preferred_element_type=F32)


def triangle(left_ref, own_ref, inverse_ref, hat_ref):
    packed = left_ref[...]
    both = products(packed.T, packed)
    gram = both[:RANK, :RANK] + both[RANK:, RANK:]
    row = lax.broadcasted_iota(jnp.int32, (RANK, RANK), 0)
    diagonal = row == lax.broadcasted_iota(jnp.int32, (RANK, RANK), 1)
    shift = 0.01 * (jnp.sum(jnp.where(diagonal, gram, 0.0)) / RANK + 1e-06)
    eye = jnp.where(diagonal, 1.0, 0.0)
    work = jnp.concatenate([gram + shift * eye, eye], axis=1)
    below = lax.broadcasted_iota(jnp.int32, (RANK, 1), 0)
    scale = jnp.zeros((RANK, 1), F32)
    for k in range(RANK):
        column, line = work[:, k : k + 1], work[k : k + 1]
        pivot = line[:, k : k + 1]
        scale = jnp.where(below == k, pivot, scale)
        work = work - jnp.where(below > k, column / pivot, 0.0) * line
    inverse = work[:, RANK:] * lax.rsqrt(scale)
    inverse_ref[...] = inverse / (NY * NC)
    hat_ref[...] = lax.dot_general(
        own_ref[...], inverse, (((1,), (1,)), ((), ())), precision=HIGHEST, preferred_element_type=F32
    )


def apply(blocks_ref, inverse_ref, q_ref):
    for k in range(blocks_ref.shape[0]):
        q_ref[k] = products(inverse_ref[...], blocks_ref[k])


def finish(s_ref, mine_ref, other_ref, left_ref, weight_ref, q_ref, approx_out, weight_out):
    step = pl.program_id(0)
    cols = mine_ref.shape[2]

    def run(blocks_ref):
        for k in range(blocks_ref.shape[0]):
            at = slice(k * cols, (k + 1) * cols)
            block = blocks_ref[k]
            q_ref[:, at] = block
            approx = products(left_ref[...], block)
            approx_out[:, at] = approx
            weight_out[:, at] = weight_ref[:, at] - 0.5 * approx

    pl.when(step == s_ref[1])(functools.partial(run, mine_ref))
    pl.when(step != s_ref[1])(functools.partial(run, other_ref))


def call(kernel, room, grid, in_specs, out_specs, out_shape, scratch=()):
    return pl.pallas_call(
        kernel,
        out_shape=out_shape,
        grid_spec=pltpu.PrefetchScalarGridSpec(
            num_scalar_prefetch=1, grid=grid, in_specs=in_specs, out_specs=out_specs, scratch_shapes=list(scratch)
        ),
        compiler_params=pltpu.CompilerParams(vmem_limit_bytes=room * MIB),
    )


def whole(shape):
    return pl.BlockSpec(shape, lambda *_: (0,) * len(shape))


def on_device(grad_terms, error_buffer, weight, q_prev):
    term, error = grad_terms[0, 0], error_buffer[0]
    rows, width = term.shape
    half, cols = rows // 2, width // (NY * NC)
    array = lambda *shape: jax.ShapeDtypeStruct(shape, F32)
    core = lax.axis_index("core")
    place = jnp.stack([lax.axis_index("z") * NX + lax.axis_index("x"), core]).astype(jnp.int32)

    bands = NZ // 2
    anywhere = pl.BlockSpec(memory_space=pl.ANY)
    wide = pl.pallas_call(
        widen,
        out_shape=array(NX, NZ, OWN, width),
        in_specs=[anywhere],
        out_specs=anywhere,
        scratch_shapes=[
            pltpu.VMEM((bands, rows // bands, width), BF16),
            pltpu.VMEM((bands, NX, NZ // bands, OWN, width), F32),
            pltpu.SemaphoreType.DMA((bands,)),
            pltpu.SemaphoreType.DMA((bands,)),
        ],
        compiler_params=pltpu.CompilerParams(vmem_limit_bytes=60 * MIB),
    )(term)
    left = pl.pallas_call(
        left_terms,
        out_shape=array(half, LANES),
        grid=(2,),
        in_specs=[pl.BlockSpec((half, width), lambda i: (i, 0)), whole((OWN, width)), whole((RANK, width))],
        out_specs=whole((half, LANES)),
        scratch_shapes=[pltpu.VMEM((3 * RANK, width), BF16)],
        compiler_params=pltpu.CompilerParams(vmem_limit_bytes=60 * MIB),
    )(term, error, q_prev.T)

    tile = exchange(left.reshape(NZ * NC, half // (NZ * NC), LANES), ("z", "core")).sum(0)
    tile = gathered(tile, ("y", "x"), NY * NX).sum(0)
    left = gathered(tile, ("z", "core"), NZ * NC).reshape(half, LANES)

    send, keep, left_own = call(
        right_terms,
        24,
        (4,),
        [
            whole((half, LANES)),
            pl.BlockSpec((rows, width // 4), lambda i, s: (0, (i + 2 - 2 * s[1]) % 4)),
            pl.BlockSpec((OWN, width // 4), lambda i, s: (0, (i + 2 - 2 * s[1]) % 4)),
        ],
        [
            pl.BlockSpec((NY // 2, RANK, cols), lambda i, _: (jnp.minimum(i, 1), 0, 0)),
            pl.BlockSpec((NY // 2, RANK, cols), lambda i, _: (jnp.maximum(i - 2, 0), 0, 0)),
            whole((OWN, RANK)),
        ],
        [array(NY, RANK, cols), array(NY, RANK, cols), array(OWN, RANK)],
        [pltpu.VMEM((2, 3 * RANK, half), BF16), pltpu.VMEM((RANK, len(PAIRS) * OWN), BF16)],
    )(place, left, term, error)
    half_sum = keep + swap(send)

    inverse, left_hat = pl.pallas_call(
        triangle,
        out_shape=(array(RANK, RANK), array(OWN, RANK)),
        compiler_params=pltpu.CompilerParams(vmem_limit_bytes=8 * MIB),
        cost_estimate=pl.CostEstimate(flops=20 * 10**9, bytes_accessed=4 * half * LANES, transcendentals=RANK),
    )(left, left_own)

    summed = scatter(wide.reshape(rows, width), "x")
    summed = pl.pallas_call(
        hand_on,
        out_shape=array(*summed.shape),
        in_specs=[anywhere, anywhere],
        out_specs=anywhere,
        input_output_aliases={1: 0},
        compiler_params=pltpu.CompilerParams(vmem_limit_bytes=60 * MIB),
    )(half_sum, summed)
    summed = scatter(summed, "z")

    block = exchange(half_sum.reshape(NY * NX, RANK // NX, cols), ("y", "x")).sum(0)
    block = gathered(block, "z", NZ).sum(0)
    mine = pl.pallas_call(
        apply,
        out_shape=array(NY, RANK, cols),
        compiler_params=pltpu.CompilerParams(vmem_limit_bytes=8 * MIB),
    )(gathered(block, ("y", "x"), NY * NX).reshape(NY, RANK, cols), inverse)
    other = swap(mine)
    side = pl.BlockSpec((OWN, width // 2), lambda i, _: (0, i))
    q_turned, approx, weight_next = call(
        finish,
        16,
        (2,),
        [whole((NY, RANK, cols)), whole((NY, RANK, cols)), whole((OWN, RANK)), side],
        [pl.BlockSpec((RANK, width // 2), lambda i, _: (0, i)), side, side],
        [array(RANK, width), array(OWN, width), array(OWN, width)],
    )(place, mine, other, left_hat, weight)
    return (q_turned.T, (summed + error - approx)[None], weight_next)


def solution(mesh):
    split = Mesh(mesh.devices.reshape(NY, NC, NZ, NX), REP + GRP)
    placed = (P(REP, GRP, None, None), P(REP, GRP, None), P(GRP, None), P())
    return jax.shard_map(
        on_device,
        mesh=split,
        in_specs=placed,
        out_specs=(P(), P(REP, GRP, None), P(GRP, None)),
        check_vma=False,
    )
```

```python
import functools

import jax
import jax.numpy as jnp
from jax import lax
from jax.experimental import pallas as pl
from jax.experimental.pallas import tpu as pltpu
from jax.sharding import Mesh, PartitionSpec as P

NY, NC, NZ, NX = 8, 2, 12, 4
REP, GRP = ("y", "core"), ("z", "x")
F32, BF16 = jnp.float32, jnp.bfloat16
RANK, OWN, LANES = 64, 8, 128
HIGHEST = lax.Precision.HIGHEST
MIB = 2**20
PAIRS = ((0, 0), (0, 1), (1, 0), (1, 1), (0, 2), (2, 0))


def parts_of(value):
    high = value.astype(BF16).astype(F32)
    rest = value - high
    middle = rest.astype(BF16).astype(F32)
    return [high, middle, rest - middle]


def stacked(parts):
    return jnp.concatenate(parts, axis=0).astype(BF16)


def dot_nt(left, right):
    return lax.dot_general(left, right, (((1,), (1,)), ((), ())), preferred_element_type=F32)


def exchange(value, axes):
    return lax.all_to_all(value, axes, 0, 0, tiled=True)


def gathered(value, axes, n):
    return exchange(jnp.broadcast_to(value[None], (n,) + value.shape), axes)


def scatter(value, axis):
    return lax.psum_scatter(value, axis, scatter_dimension=0, tiled=True)


def swap(value):
    return lax.ppermute(value, "core", [(i, NC - 1 - i) for i in range(NC)])


def own_place(g, n_tiles):
    low = g < n_tiles
    return low, pl.multiple_of(jnp.where(low, g, g - n_tiles) * OWN, OWN)


def widen(term_ref, wide_ref, narrow, wide, arrived, left):
    bands = narrow.shape[0]
    per = NZ // bands
    size = per * NX * OWN
    reads = [pltpu.make_async_copy(term_ref.at[pl.ds(i * size, size)], narrow.at[i], arrived.at[i]) for i in range(bands)]
    writes = [pltpu.make_async_copy(wide.at[i], wide_ref.at[:, pl.ds(i * per, per)], left.at[i]) for i in range(bands)]
    for copy in reads:
        copy.start()
    for i in range(bands):
        reads[i].wait()
        block = narrow[i].astype(F32)
        for z in range(per):
            for x in range(NX):
                at = (z * NX + x) * OWN
                wide[i, x, z] = block[at : at + OWN]
        writes[i].start()
    for copy in writes:
        copy.wait()


def left_terms(term_ref, error_ref, q_ref, left_ref, parts):
    step = pl.program_id(0)
    rows = term_ref.shape[0]

    @pl.when(step == 0)
    def _():
        for i, part in enumerate(parts_of(q_ref[...])):
            parts[i * RANK : (i + 1) * RANK] = part.astype(BF16)

    product = dot_nt(term_ref[...], parts[...])
    left = product[:, :RANK] + product[:, RANK : 2 * RANK] + product[:, 2 * RANK :]

    @pl.when(step == 0)
    def _():
        left_ref[:, :RANK] = left

    @pl.when(step == 1)
    def _():
        left_ref[:, RANK:] = left
        high, middle, low = parts_of(error_ref[...])
        errors = stacked([high, middle, low, jnp.zeros_like(low)])
        cross = dot_nt(errors, parts[...])
        own = cross[2 * OWN : 3 * OWN, :RANK] + cross[:OWN, 2 * RANK :]
        own = own + cross[OWN : 2 * OWN, RANK : 2 * RANK]
        own = own + cross[OWN : 2 * OWN, :RANK] + cross[:OWN, RANK : 2 * RANK]
        own = own + cross[:OWN, :RANK]
        first, at = own_place(lax.axis_index("z") * NX + lax.axis_index("x"), rows // OWN)
        none = jnp.zeros_like(own)
        pair = jnp.concatenate([jnp.where(first, own, none), jnp.where(first, none, own)], axis=1)
        left_ref[pl.ds(at, OWN), :] += pair


def right_terms(s_ref, left_ref, term_ref, error_ref, send_ref, keep_ref, own_ref, parts, own_parts):
    step = pl.program_id(0)
    half = term_ref.shape[0] // 2
    first, at = own_place(s_ref[0], half // OWN)

    @pl.when(step == 0)
    def _():
        turned = left_ref[...].T
        for i in range(2):
            for j, part in enumerate(parts_of(turned[i * RANK : (i + 1) * RANK])):
                parts[i, j * RANK : (j + 1) * RANK] = part.astype(BF16)
        pair = left_ref[pl.ds(at, OWN), :]
        own = jnp.where(first, pair[:, :RANK], pair[:, RANK:])
        own_ref[...] = own
        cut = parts_of(own)
        own_parts[...] = jnp.concatenate([cut[i] for i, _ in PAIRS], axis=0).T.astype(BF16)

    total = jnp.dot(parts[0], term_ref[:half], preferred_element_type=F32)
    total = total + jnp.dot(parts[1], term_ref[half:], preferred_element_type=F32)
    total = total[:RANK] + total[RANK : 2 * RANK] + total[2 * RANK :]
    cut = parts_of(error_ref[...])
    total = total + jnp.dot(own_parts[...], stacked([cut[j] for _, j in PAIRS]), preferred_element_type=F32)
    count, cols = send_ref.shape[0], send_ref.shape[2]

    @pl.when(step < 2)
    def _():
        for k in range(count):
            send_ref[k] = total[:, k * cols : (k + 1) * cols]

    @pl.when(step >= 2)
    def _():
        for k in range(count):
            keep_ref[k] = total[:, k * cols : (k + 1) * cols]


def hand_on(_, __, ___):
    pass


def products(left, right):
    a, b = parts_of(left), parts_of(right)
    wide = jnp.concatenate([a[i] for i, _ in PAIRS], axis=1).astype(BF16)
    return jnp.dot(wide, stacked([b[j] for _, j in PAIRS]), preferred_element_type=F32)


def triangle(left_ref, own_ref, inverse_ref, hat_ref):
    packed = left_ref[...]
    both = products(packed.T, packed)
    gram = both[:RANK, :RANK] + both[RANK:, RANK:]
    row = lax.broadcasted_iota(jnp.int32, (RANK, RANK), 0)
    diagonal = row == lax.broadcasted_iota(jnp.int32, (RANK, RANK), 1)
    shift = 0.01 * (jnp.sum(jnp.where(diagonal, gram, 0.0)) / RANK + 1e-06)
    eye = jnp.where(diagonal, 1.0, 0.0)
    work = jnp.concatenate([gram + shift * eye, eye], axis=1)
    below = lax.broadcasted_iota(jnp.int32, (RANK, 1), 0)
    scale = jnp.zeros((RANK, 1), F32)
    for k in range(RANK):
        column, line = work[:, k : k + 1], work[k : k + 1]
        pivot = line[:, k : k + 1]
        scale = jnp.where(below == k, pivot, scale)
        work = work - jnp.where(below > k, column / pivot, 0.0) * line
    inverse = work[:, RANK:] * lax.rsqrt(scale)
    inverse_ref[...] = inverse / (NY * NC)
    hat_ref[...] = lax.dot_general(
        own_ref[...], inverse, (((1,), (1,)), ((), ())), precision=HIGHEST, preferred_element_type=F32
    )


def apply(blocks_ref, inverse_ref, q_ref):
    for k in range(blocks_ref.shape[0]):
        q_ref[k] = products(inverse_ref[...], blocks_ref[k])


def finish(s_ref, mine_ref, other_ref, left_ref, error_ref, weight_ref, q_ref, change_out, weight_out):
    step = pl.program_id(0)
    cols = mine_ref.shape[2]

    def run(blocks_ref):
        for k in range(blocks_ref.shape[0]):
            at = slice(k * cols, (k + 1) * cols)
            block = blocks_ref[k]
            q_ref[:, at] = block
            approx = products(left_ref[...], block)
            change_out[:, at] = error_ref[:, at] - approx
            weight_out[:, at] = weight_ref[:, at] - 0.5 * approx

    pl.when(step == s_ref[1])(functools.partial(run, mine_ref))
    pl.when(step != s_ref[1])(functools.partial(run, other_ref))


def call(kernel, room, grid, in_specs, out_specs, out_shape, scratch=()):
    return pl.pallas_call(
        kernel,
        out_shape=out_shape,
        grid_spec=pltpu.PrefetchScalarGridSpec(
            num_scalar_prefetch=1, grid=grid, in_specs=in_specs, out_specs=out_specs, scratch_shapes=list(scratch)
        ),
        compiler_params=pltpu.CompilerParams(vmem_limit_bytes=room * MIB),
    )


def whole(shape):
    return pl.BlockSpec(shape, lambda *_: (0,) * len(shape))


def on_device(grad_terms, error_buffer, weight, q_prev):
    term, error = grad_terms[0, 0], error_buffer[0]
    rows, width = term.shape
    half, cols = rows // 2, width // (NY * NC)
    array = lambda *shape: jax.ShapeDtypeStruct(shape, F32)
    core = lax.axis_index("core")
    place = jnp.stack([lax.axis_index("z") * NX + lax.axis_index("x"), core]).astype(jnp.int32)

    bands = NZ
    anywhere = pl.BlockSpec(memory_space=pl.ANY)
    wide = pl.pallas_call(
        widen,
        out_shape=array(NX, NZ, OWN, width),
        in_specs=[anywhere],
        out_specs=anywhere,
        scratch_shapes=[
            pltpu.VMEM((bands, rows // bands, width), BF16),
            pltpu.VMEM((bands, NX, NZ // bands, OWN, width), F32),
            pltpu.SemaphoreType.DMA((bands,)),
            pltpu.SemaphoreType.DMA((bands,)),
        ],
        compiler_params=pltpu.CompilerParams(vmem_limit_bytes=60 * MIB),
    )(term)
    left = pl.pallas_call(
        left_terms,
        out_shape=array(half, LANES),
        grid=(2,),
        in_specs=[pl.BlockSpec((half, width), lambda i: (i, 0)), whole((OWN, width)), whole((RANK, width))],
        out_specs=whole((half, LANES)),
        scratch_shapes=[pltpu.VMEM((3 * RANK, width), BF16)],
        compiler_params=pltpu.CompilerParams(vmem_limit_bytes=60 * MIB),
    )(term, error, q_prev.T)

    tile = exchange(left.reshape(NZ * NC, half // (NZ * NC), LANES), ("z", "core")).sum(0)
    tile = gathered(tile, ("y", "x"), NY * NX).sum(0)
    left = gathered(tile, ("z", "core"), NZ * NC).reshape(half, LANES)

    send, keep, left_own = call(
        right_terms,
        24,
        (4,),
        [
            whole((half, LANES)),
            pl.BlockSpec((rows, width // 4), lambda i, s: (0, (i + 2 - 2 * s[1]) % 4)),
            pl.BlockSpec((OWN, width // 4), lambda i, s: (0, (i + 2 - 2 * s[1]) % 4)),
        ],
        [
            pl.BlockSpec((NY // 2, RANK, cols), lambda i, _: (jnp.minimum(i, 1), 0, 0)),
            pl.BlockSpec((NY // 2, RANK, cols), lambda i, _: (jnp.maximum(i - 2, 0), 0, 0)),
            whole((OWN, RANK)),
        ],
        [array(NY, RANK, cols), array(NY, RANK, cols), array(OWN, RANK)],
        [pltpu.VMEM((2, 3 * RANK, half), BF16), pltpu.VMEM((RANK, len(PAIRS) * OWN), BF16)],
    )(place, left, term, error)
    half_sum = keep + swap(send)

    inverse, left_hat = pl.pallas_call(
        triangle,
        out_shape=(array(RANK, RANK), array(OWN, RANK)),
        compiler_params=pltpu.CompilerParams(vmem_limit_bytes=8 * MIB),
        cost_estimate=pl.CostEstimate(flops=20 * 10**9, bytes_accessed=4 * half * LANES, transcendentals=RANK),
    )(left, left_own)

    summed = scatter(wide.reshape(rows, width), "x")
    summed = pl.pallas_call(
        hand_on,
        out_shape=array(*summed.shape),
        in_specs=[anywhere, anywhere],
        out_specs=anywhere,
        input_output_aliases={1: 0},
        compiler_params=pltpu.CompilerParams(vmem_limit_bytes=60 * MIB),
    )(half_sum, summed)
    summed = scatter(summed, "z")

    block = exchange(half_sum.reshape(NY * NX, RANK // NX, cols), ("y", "x")).sum(0)
    block = gathered(block, "z", NZ).sum(0)
    mine = pl.pallas_call(
        apply,
        out_shape=array(NY, RANK, cols),
        compiler_params=pltpu.CompilerParams(vmem_limit_bytes=8 * MIB),
    )(gathered(block, ("y", "x"), NY * NX).reshape(NY, RANK, cols), inverse)
    other = swap(mine)
    side = pl.BlockSpec((OWN, width // 2), lambda i, _: (0, i))
    q_turned, change, weight_next = call(
        finish,
        16,
        (2,),
        [whole((NY, RANK, cols)), whole((NY, RANK, cols)), whole((OWN, RANK)), side, side],
        [pl.BlockSpec((RANK, width // 2), lambda i, _: (0, i)), side, side],
        [array(RANK, width), array(OWN, width), array(OWN, width)],
    )(place, mine, other, left_hat, error, weight)
    return (q_turned.T, (summed + change)[None], weight_next)


def solution(mesh):
    split = Mesh(mesh.devices.reshape(NY, NC, NZ, NX), REP + GRP)
    placed = (P(REP, GRP, None, None), P(REP, GRP, None), P(GRP, None), P())
    return jax.shard_map(
        on_device,
        mesh=split,
        in_specs=placed,
        out_specs=(P(), P(REP, GRP, None), P(GRP, None)),
        check_vma=False,
    )
```

```python
import functools

import jax
import jax.numpy as jnp
from jax import lax
from jax.experimental import pallas as pl
from jax.experimental.pallas import tpu as pltpu
from jax.sharding import Mesh, PartitionSpec as P

NY, NC, NZ, NX = 8, 2, 12, 4
REP, GRP = ("y", "core"), ("z", "x")
F32, BF16 = jnp.float32, jnp.bfloat16
RANK, OWN, LANES = 64, 8, 128
HIGHEST = lax.Precision.HIGHEST
MIB = 2**20
PAIRS = ((0, 0), (0, 1), (1, 0), (1, 1), (0, 2), (2, 0))


def parts_of(value):
    high = value.astype(BF16).astype(F32)
    rest = value - high
    middle = rest.astype(BF16).astype(F32)
    return [high, middle, rest - middle]


def stacked(parts):
    return jnp.concatenate(parts, axis=0).astype(BF16)


def dot_nt(left, right):
    return lax.dot_general(left, right, (((1,), (1,)), ((), ())), preferred_element_type=F32)


def exchange(value, axes):
    return lax.all_to_all(value, axes, 0, 0, tiled=True)


def gathered(value, axes, n):
    return exchange(jnp.broadcast_to(value[None], (n,) + value.shape), axes)


def scatter(value, axis):
    return lax.psum_scatter(value, axis, scatter_dimension=0, tiled=True)


def swap(value):
    return lax.ppermute(value, "core", [(i, NC - 1 - i) for i in range(NC)])


def own_place(g, n_tiles):
    low = g < n_tiles
    return low, pl.multiple_of(jnp.where(low, g, g - n_tiles) * OWN, OWN)


def widen(term_ref, wide_ref, narrow, wide, arrived, left):
    bands = narrow.shape[0]
    per = NZ // bands
    size = per * NX * OWN
    reads = [pltpu.make_async_copy(term_ref.at[pl.ds(i * size, size)], narrow.at[i], arrived.at[i]) for i in range(bands)]
    writes = [pltpu.make_async_copy(wide.at[i], wide_ref.at[:, pl.ds(i * per, per)], left.at[i]) for i in range(bands)]
    for copy in reads:
        copy.start()
    for i in range(bands):
        reads[i].wait()
        block = narrow[i].astype(F32)
        for z in range(per):
            for x in range(NX):
                at = (z * NX + x) * OWN
                wide[i, x, z] = block[at : at + OWN]
        writes[i].start()
    for copy in writes:
        copy.wait()


def left_terms(term_ref, error_ref, q_ref, left_ref, parts):
    step = pl.program_id(0)
    rows = term_ref.shape[0]

    @pl.when(step == 0)
    def _():
        for i, part in enumerate(parts_of(q_ref[...])):
            parts[i * RANK : (i + 1) * RANK] = part.astype(BF16)

    product = dot_nt(term_ref[...], parts[...])
    left = product[:, :RANK] + product[:, RANK : 2 * RANK] + product[:, 2 * RANK :]

    @pl.when(step == 0)
    def _():
        left_ref[:, :RANK] = left

    @pl.when(step == 1)
    def _():
        left_ref[:, RANK:] = left
        high, middle, low = parts_of(error_ref[...])
        errors = stacked([high, middle, low, jnp.zeros_like(low)])
        cross = dot_nt(errors, parts[...])
        own = cross[2 * OWN : 3 * OWN, :RANK] + cross[:OWN, 2 * RANK :]
        own = own + cross[OWN : 2 * OWN, RANK : 2 * RANK]
        own = own + cross[OWN : 2 * OWN, :RANK] + cross[:OWN, RANK : 2 * RANK]
        own = own + cross[:OWN, :RANK]
        first, at = own_place(lax.axis_index("z") * NX + lax.axis_index("x"), rows // OWN)
        none = jnp.zeros_like(own)
        pair = jnp.concatenate([jnp.where(first, own, none), jnp.where(first, none, own)], axis=1)
        left_ref[pl.ds(at, OWN), :] += pair


def right_terms(s_ref, left_ref, term_ref, error_ref, send_ref, keep_ref, own_ref, parts, own_parts):
    step = pl.program_id(0)
    half = term_ref.shape[0] // 2
    first, at = own_place(s_ref[0], half // OWN)

    @pl.when(step == 0)
    def _():
        turned = left_ref[...].T
        for i in range(2):
            for j, part in enumerate(parts_of(turned[i * RANK : (i + 1) * RANK])):
                parts[i, j * RANK : (j + 1) * RANK] = part.astype(BF16)
        pair = left_ref[pl.ds(at, OWN), :]
        own = jnp.where(first, pair[:, :RANK], pair[:, RANK:])
        own_ref[...] = own
        cut = parts_of(own)
        own_parts[...] = jnp.concatenate([cut[i] for i, _ in PAIRS], axis=0).T.astype(BF16)

    total = jnp.dot(parts[0], term_ref[:half], preferred_element_type=F32)
    total = total + jnp.dot(parts[1], term_ref[half:], preferred_element_type=F32)
    total = total[:RANK] + total[RANK : 2 * RANK] + total[2 * RANK :]
    cut = parts_of(error_ref[...])
    total = total + jnp.dot(own_parts[...], stacked([cut[j] for _, j in PAIRS]), preferred_element_type=F32)
    count, cols = send_ref.shape[0], send_ref.shape[2]

    @pl.when(step < 2)
    def _():
        for k in range(count):
            send_ref[k] = total[:, k * cols : (k + 1) * cols]

    @pl.when(step >= 2)
    def _():
        for k in range(count):
            keep_ref[k] = total[:, k * cols : (k + 1) * cols]


def hand_on(_, __, ___):
    pass


def products(left, right):
    a, b = parts_of(left), parts_of(right)
    wide = jnp.concatenate([a[i] for i, _ in PAIRS], axis=1).astype(BF16)
    return jnp.dot(wide, stacked([b[j] for _, j in PAIRS]), preferred_element_type=F32)


def triangle(left_ref, own_ref, inverse_ref, hat_ref):
    packed = left_ref[...]
    both = products(packed.T, packed)
    gram = both[:RANK, :RANK] + both[RANK:, RANK:]
    row = lax.broadcasted_iota(jnp.int32, (RANK, RANK), 0)
    diagonal = row == lax.broadcasted_iota(jnp.int32, (RANK, RANK), 1)
    shift = 0.01 * (jnp.sum(jnp.where(diagonal, gram, 0.0)) / RANK + 1e-06)
    eye = jnp.where(diagonal, 1.0, 0.0)
    work = jnp.concatenate([gram + shift * eye, eye], axis=1)
    below = lax.broadcasted_iota(jnp.int32, (RANK, 1), 0)
    scale = jnp.zeros((RANK, 1), F32)
    for k in range(RANK):
        column, line = work[:, k : k + 1], work[k : k + 1]
        pivot = line[:, k : k + 1]
        scale = jnp.where(below == k, pivot, scale)
        work = work - jnp.where(below > k, column / pivot, 0.0) * line
    inverse = work[:, RANK:] * lax.rsqrt(scale)
    inverse_ref[...] = inverse / (NY * NC)
    hat_ref[...] = lax.dot_general(
        own_ref[...], inverse, (((1,), (1,)), ((), ())), precision=HIGHEST, preferred_element_type=F32
    )


def apply(blocks_ref, inverse_ref, q_ref):
    for k in range(blocks_ref.shape[0]):
        q_ref[k] = products(inverse_ref[...], blocks_ref[k])


def finish(s_ref, mine_ref, other_ref, left_ref, error_ref, weight_ref, q_ref, change_out, weight_out):
    step = pl.program_id(0)
    cols = mine_ref.shape[2]

    def run(blocks_ref):
        for k in range(blocks_ref.shape[0]):
            at = slice(k * cols, (k + 1) * cols)
            block = blocks_ref[k]
            q_ref[:, at] = block
            approx = products(left_ref[...], block)
            change_out[:, at] = error_ref[:, at] - approx
            weight_out[:, at] = weight_ref[:, at] - 0.5 * approx

    pl.when(step == s_ref[1])(functools.partial(run, mine_ref))
    pl.when(step != s_ref[1])(functools.partial(run, other_ref))


def call(kernel, room, grid, in_specs, out_specs, out_shape, scratch=()):
    return pl.pallas_call(
        kernel,
        out_shape=out_shape,
        grid_spec=pltpu.PrefetchScalarGridSpec(
            num_scalar_prefetch=1, grid=grid, in_specs=in_specs, out_specs=out_specs, scratch_shapes=list(scratch)
        ),
        compiler_params=pltpu.CompilerParams(vmem_limit_bytes=room * MIB),
    )


def whole(shape):
    return pl.BlockSpec(shape, lambda *_: (0,) * len(shape))


def on_device(grad_terms, error_buffer, weight, q_prev):
    term, error = grad_terms[0, 0], error_buffer[0]
    rows, width = term.shape
    half, cols = rows // 2, width // (NY * NC)
    array = lambda *shape: jax.ShapeDtypeStruct(shape, F32)
    core = lax.axis_index("core")
    place = jnp.stack([lax.axis_index("z") * NX + lax.axis_index("x"), core]).astype(jnp.int32)

    bands = NZ
    anywhere = pl.BlockSpec(memory_space=pl.ANY)
    wide = pl.pallas_call(
        widen,
        out_shape=array(NX, NZ, OWN, width),
        in_specs=[anywhere],
        out_specs=anywhere,
        scratch_shapes=[
            pltpu.VMEM((bands, rows // bands, width), BF16),
            pltpu.VMEM((bands, NX, NZ // bands, OWN, width), F32),
            pltpu.SemaphoreType.DMA((bands,)),
            pltpu.SemaphoreType.DMA((bands,)),
        ],
        compiler_params=pltpu.CompilerParams(vmem_limit_bytes=60 * MIB),
    )(term)
    left = pl.pallas_call(
        left_terms,
        out_shape=array(half, LANES),
        grid=(2,),
        in_specs=[pl.BlockSpec((half, width), lambda i: (i, 0)), whole((OWN, width)), whole((RANK, width))],
        out_specs=whole((half, LANES)),
        scratch_shapes=[pltpu.VMEM((3 * RANK, width), BF16)],
        compiler_params=pltpu.CompilerParams(vmem_limit_bytes=60 * MIB),
    )(term, error, q_prev.T)

    tile = exchange(left.reshape(NZ * NC, half // (NZ * NC), LANES), ("z", "core")).sum(0)
    tile = gathered(tile, ("y", "x"), NY * NX).sum(0)
    left = gathered(tile, ("z", "core"), NZ * NC).reshape(half, LANES)

    send, keep, left_own = call(
        right_terms,
        24,
        (4,),
        [
            whole((half, LANES)),
            pl.BlockSpec((rows, width // 4), lambda i, s: (0, (i + 2 - 2 * s[1]) % 4)),
            pl.BlockSpec((OWN, width // 4), lambda i, s: (0, (i + 2 - 2 * s[1]) % 4)),
        ],
        [
            pl.BlockSpec((NY // 2, RANK, cols), lambda i, _: (jnp.minimum(i, 1), 0, 0)),
            pl.BlockSpec((NY // 2, RANK, cols), lambda i, _: (jnp.maximum(i - 2, 0), 0, 0)),
            whole((OWN, RANK)),
        ],
        [array(NY, RANK, cols), array(NY, RANK, cols), array(OWN, RANK)],
        [pltpu.VMEM((2, 3 * RANK, half), BF16), pltpu.VMEM((RANK, len(PAIRS) * OWN), BF16)],
    )(place, left, term, error)
    half_sum = keep + swap(send)

    inverse, left_hat = pl.pallas_call(
        triangle,
        out_shape=(array(RANK, RANK), array(OWN, RANK)),
        compiler_params=pltpu.CompilerParams(vmem_limit_bytes=8 * MIB),
        cost_estimate=pl.CostEstimate(flops=4 * RANK**3, bytes_accessed=4 * half * LANES, transcendentals=RANK),
    )(left, left_own)

    summed = scatter(wide.reshape(rows, width), "x")
    summed = pl.pallas_call(
        hand_on,
        out_shape=array(*summed.shape),
        in_specs=[anywhere, anywhere],
        out_specs=anywhere,
        input_output_aliases={1: 0},
        compiler_params=pltpu.CompilerParams(vmem_limit_bytes=60 * MIB),
    )(half_sum, summed)
    summed = scatter(summed, "z")

    block = exchange(half_sum.reshape(NY * NX, RANK // NX, cols), ("y", "x")).sum(0)
    block = gathered(block, "z", NZ).sum(0)
    mine = pl.pallas_call(
        apply,
        out_shape=array(NY, RANK, cols),
        compiler_params=pltpu.CompilerParams(vmem_limit_bytes=8 * MIB),
    )(gathered(block, ("y", "x"), NY * NX).reshape(NY, RANK, cols), inverse)
    other = swap(mine)
    side = pl.BlockSpec((OWN, width // 2), lambda i, _: (0, i))
    q_turned, change, weight_next = call(
        finish,
        16,
        (2,),
        [whole((NY, RANK, cols)), whole((NY, RANK, cols)), whole((OWN, RANK)), side, side],
        [pl.BlockSpec((RANK, width // 2), lambda i, _: (0, i)), side, side],
        [array(RANK, width), array(OWN, width), array(OWN, width)],
    )(place, mine, other, left_hat, error, weight)
    return (q_turned.T, (summed + change)[None], weight_next)


def solution(mesh):
    split = Mesh(mesh.devices.reshape(NY, NC, NZ, NX), REP + GRP)
    placed = (P(REP, GRP, None, None), P(REP, GRP, None), P(GRP, None), P())
    return jax.shard_map(
        on_device,
        mesh=split,
        in_specs=placed,
        out_specs=(P(), P(REP, GRP, None), P(GRP, None)),
        check_vma=False,
    )
```
